32 devices in a mesh: groups: 2 (over x), row: 16 (over z, y, core).
Axes of the slice: x: 2, y: 2, z: 4, core: 2. Of those that a mesh axis runs over, the one named last changes fastest.
Arguments:
- left_alignment: bfloat16 [64, 4096], P('groups', 'row'), parts along dimension 0, may hold values from -12 to 12
- right_alignment: bfloat16 [64, 4096], P('groups', 'row'), parts along dimension 0, may hold values from -12 to 12
- pair_update_gradient: bfloat16 [256, 128, 128], P(('groups', 'row')), parts along dimension 0, may hold values from -6 to 6
- weight: bfloat16 [1024, 128], replicated, may hold values from -0.1875 to 0.1875
- bias: bfloat16 [128], replicated, may hold values from -3 to 3
Outputs:
- pair_update: bfloat16 [256, 128, 128], P(('groups', 'row')), parts along dimension 0
- grad_left: float32 [64, 4096], P('groups', 'row'), parts along dimension 0
- grad_right: float32 [64, 4096], P('groups', 'row'), parts along dimension 0
- grad_weight: float32 [2048, 128], P('groups'), parts along dimension 0
- grad_bias: float32 [256], P('groups'), parts along dimension 0
The draws below stay inside these ranges and needn't reach their ends.
There are 2 independent parts, one for each index of `groups`. The reference program is written for one: setup_inputs(seed, part) draws one part's arguments, and reference() takes and returns one part's arrays. A program takes and returns all parts, laid end to end along the dimension named above; an argument that names none is the same for every part. Nothing has to cross between parts.
All inputs are finite; a program needn't handle non-finite values.
Results may differ from the reference program's by a relative error of at most 0.0043.
Values may be sent and summed in bfloat16 or wider, within the bound.
A program may use at most 128 MiB of HBM per device.

```python
import jax
import jax.numpy as jnp
from jax import lax

CHANNEL_WIDTH = 32
CZ = 128
SEQUENCE_COUNT = 32
K = 1024
RESIDUE_COUNT = 128


def raised(entries, own_key, source, target, blocks, factor):
    def block_of(position):
        return (jnp.arange(entries.shape[position]) // (entries.shape[position] // blocks)).reshape((-1,) + (1,) * (entries.ndim - 1 - position))

    near = jax.random.permutation(own_key, blocks)[block_of(target)]
    far = (block_of(target) + blocks // 2) % blocks
    return jnp.where((block_of(source) == near) | (block_of(source) == far), factor * entries, entries)


def levels(stream_key, shape, split, low, top_value):
    gain = 1.0
    for dim, parts in split:
        draws = jax.random.uniform(jax.random.fold_in(jax.random.fold_in(stream_key, 6), dim), (parts,), jnp.float32, low / len(split), top_value / len(split))
        gain = gain * jnp.repeat(jnp.exp(draws), shape[dim] // parts).reshape((-1,) + (1,) * (len(shape) - 1 - dim))
    return gain


def gaussian(own_key, extent, scale, limit, cuts=(), held_as=jnp.bfloat16):
    result = jax.random.normal(own_key, extent, jnp.float32) * scale
    if len(cuts) > 0:
        result = levels(own_key, extent, cuts, -0.22, 0.18) * result
    return jnp.clip(result, min=-limit, max=limit).astype(held_as)


def gaussian_with(rng, shape, deviation, limit, shards, heavy, held_as=jnp.bfloat16):
    array = deviation * jax.random.normal(rng, shape, jnp.float32)
    if shards:
        array = array * levels(rng, shape, shards, -0.22, 0.18)
    return jnp.clip(raised(array, jax.random.fold_in(rng, 3), *heavy), -limit, limit).astype(held_as)


def setup_inputs(seed: int = 0, part: int = 0) -> dict:
    key_list = jax.random.split(jax.random.key(seed), 6)
    part_splits = jax.random.split(jax.random.fold_in(key_list[5], part), 6)
    return {
        "left_alignment": gaussian(part_splits[0], (SEQUENCE_COUNT, RESIDUE_COUNT * CHANNEL_WIDTH), 2.0, 12.0, ((1, 16),)),
        "right_alignment": gaussian(part_splits[1], (SEQUENCE_COUNT, RESIDUE_COUNT * CHANNEL_WIDTH), 2.0, 12.0, ((1, 16),)),
        "pair_update_gradient": gaussian_with(part_splits[2], (RESIDUE_COUNT, RESIDUE_COUNT, CZ), 1.0, 6.0, ((0, 16),), (0, 1, 16, 2.0)),
        "weight": gaussian(key_list[3], (K, CZ), K ** -0.5, 0.1875),
        "bias": gaussian(key_list[4], (CZ,), 0.5, 3.0),
    }


def reference(left_alignment, right_alignment, pair_update_gradient, weight, bias):
    sequence_count = left_alignment.shape[0]
    width = weight.shape[0]
    channel_total = CHANNEL_WIDTH
    grand_count = RESIDUE_COUNT
    depth = weight.shape[1]
    left_complete = left_alignment.astype(jnp.float32).reshape(sequence_count, grand_count, channel_total)
    right_complete = right_alignment.astype(jnp.float32).reshape(sequence_count, grand_count, channel_total)
    weight_f = weight.astype(jnp.float32)
    rows_block = 8
    count = grand_count // rows_block

    def step(carry, index):
        grad_right_acc, grad_weight_acc = carry
        offset = (index * rows_block).astype(jnp.int32)
        left_blk = lax.dynamic_slice_in_dim(left_complete, offset, rows_block, 1)
        outer = jnp.einsum("sic,sjd->ijcd", left_blk, right_complete) * (1.0 / sequence_count)
        outer = outer.astype(jnp.bfloat16).reshape(rows_block * grand_count, width)
        outer_f = outer.astype(jnp.float32)
        pair = (jnp.dot(outer_f, weight_f, preferred_element_type=jnp.float32)
                + bias.astype(jnp.float32)).astype(jnp.bfloat16)
        grad_blk = lax.dynamic_slice_in_dim(pair_update_gradient, offset, rows_block, 0)
        grad_blk = grad_blk.astype(jnp.float32).reshape(rows_block * grand_count, depth)
        inner = lax.dot_general(grad_blk, weight_f, (((1,), (1,)), ((), ())),
                                preferred_element_type=jnp.float32).astype(jnp.bfloat16)
        inner_f = inner.astype(jnp.float32).reshape(rows_block, grand_count, channel_total, channel_total)
        grad_left_blk = jnp.einsum("ijcd,sjd->sic", inner_f, right_complete) * (1.0 / sequence_count)
        grad_right_acc = grad_right_acc + jnp.einsum("ijcd,sic->sjd", inner_f, left_blk)
        grad_weight_acc = grad_weight_acc + lax.dot_general(
            outer_f, grad_blk, (((0,), (0,)), ((), ())), preferred_element_type=jnp.float32)
        return (grad_right_acc, grad_weight_acc), (pair.reshape(rows_block, grand_count, depth), grad_left_blk)

    start = (jnp.zeros((sequence_count, grand_count, channel_total), jnp.float32), jnp.zeros((width, depth), jnp.float32))
    (grad_right, grad_weight), (pairs, grad_lefts) = lax.scan(
        step, start, jnp.arange(count, dtype=jnp.int32))
    pair_update = pairs.reshape(grand_count, grand_count, depth)
    grad_left = jnp.transpose(grad_lefts, (1, 0, 2, 3)).reshape(sequence_count, grand_count * channel_total)
    grad_right = (grad_right * (1.0 / sequence_count)).reshape(sequence_count, grand_count * channel_total)
    grad_weight = grad_weight * (1.0 / grand_count)
    grad_bias = jnp.sum(pair_update_gradient.astype(jnp.float32), axis=(0, 1)) * (1.0 / grand_count)
    return pair_update, grad_left, grad_right, grad_weight, grad_bias
```

```python
import functools

import jax
import jax.numpy as jnp
from jax import lax
from jax.experimental import pallas as pl
from jax.experimental.pallas import tpu as pltpu
from jax.sharding import PartitionSpec as P

F32, BF16 = jnp.float32, jnp.bfloat16
NN = (((1,), (0,)), ((), ()))
NT = (((1,), (1,)), ((), ()))
TN = (((0,), (0,)), ((), ()))


def dot(x, y, dims=NN):
    return lax.dot_general(x, y, dims, preferred_element_type=F32)


def kernel(
    n, left, right, grad, weight, bias,
    pair_out, gl_out, gr_out, gw_out, gb_out,
    weight_f, weight_r, t_mat, u_mat, u_acc,
    bt_all, gb_all, gr_send, gr_recv, gw_send, gw_recv, gw_all,
    bt_s, bt_r, gb_s, gb_r, gr_s, gr_r, gw_s, gw_r, ga_s, ga_r,
):
    seqs = left.shape[0]
    rows, residues, depth = grad.shape
    chans = left.shape[1] // rows
    inner = chans * seqs
    span = min(128, residues)
    blocks = residues // span
    me = lax.axis_index("row")

    def peer(k):
        return lax.rem(me + k, n)

    def each_peer(action):
        def step(k, carry):
            action(peer(k))
            return carry
        lax.fori_loop(1, n, step, 0)

    def each_block(action):
        if blocks == 1:
            action(0)
        else:
            def step(k, carry):
                action(pl.multiple_of(k * span, span))
                return carry
            lax.fori_loop(0, blocks, step, 0)

    def send(buffer_from, slot_from, buffer_to, sems, remote, p):
        pltpu.make_async_remote_copy(
            src_ref=buffer_from.at[slot_from],
            dst_ref=buffer_to.at[me],
            send_sem=sems.at[p],
            recv_sem=remote.at[me],
            device_id={"row": p},
            device_id_type=pl.DeviceIdType.MESH,
        ).start()

    def wait_recv(buffer, sems, remote, p):
        pltpu.make_async_remote_copy(
            src_ref=buffer.at[p],
            dst_ref=buffer.at[p],
            send_sem=sems.at[p],
            recv_sem=remote.at[p],
            device_id={"row": p},
            device_id_type=pl.DeviceIdType.MESH,
        ).wait_recv()

    def wait_send(buffer, sems, remote, slot, p):
        pltpu.make_async_remote_copy(
            src_ref=buffer.at[slot],
            dst_ref=buffer.at[slot],
            send_sem=sems.at[p],
            recv_sem=remote.at[p],
            device_id={"row": p},
            device_id_type=pl.DeviceIdType.MESH,
        ).wait_send()

    barrier = pltpu.get_barrier_semaphore()
    each_peer(lambda p: pl.semaphore_signal(
        barrier, inc=1, device_id={"row": p}, device_id_type=pl.DeviceIdType.MESH))

    lane_s = lax.broadcasted_iota(jnp.int32, (seqs, inner), 1) % seqs
    pick = (lane_s == lax.broadcasted_iota(jnp.int32, (seqs, inner), 0)).astype(BF16)
    lane_d = lax.broadcasted_iota(jnp.int32, (rows * chans, inner), 1) // seqs
    row_d = lax.broadcasted_iota(jnp.int32, (rows * chans, inner), 0) % chans
    own = lane_d == row_d
    spread = jnp.where(own, dot(right[...], pick, TN), 0.0)
    bt_all[me] = jnp.sum(spread.reshape(rows, chans, inner), axis=1).astype(BF16)

    gb = jnp.zeros((8, depth), F32)
    for i in range(rows):
        gb = gb + jnp.sum(grad[i].astype(F32).reshape(residues // 8, 8, depth), axis=0)
    gb_all[me] = gb

    pl.semaphore_wait(barrier, n - 1)

    def send_first(p):
        send(bt_all, me, bt_all, bt_s, bt_r, p)
        send(gb_all, me, gb_all, gb_s, gb_r, p)
    each_peer(send_first)

    a = jnp.concatenate([left[:, i * chans:(i + 1) * chans] for i in range(rows)], axis=0)
    weight_f[...] = weight[...].astype(F32)
    for d in range(chans):
        weight_r[:, d * depth:(d + 1) * depth] = weight_f[
            pl.ds(d, chans, stride=chans), :].astype(BF16)

    for d in range(chans):
        t = dot(a, weight_r[:, d * depth:(d + 1) * depth]).astype(BF16)
        for i in range(rows):
            t_mat[d * seqs:(d + 1) * seqs, i * depth:(i + 1) * depth] = (
                t[i * seqs:(i + 1) * seqs])

    def grad_of(start):
        return jnp.concatenate(
            [grad[i, pl.ds(start, span), :] for i in range(rows)], axis=1)

    scale = 1.0 / seqs

    def right_share(start):
        share = dot(grad_of(start), t_mat[...], NT) * scale
        gr_send[pl.ds(start // rows, span // rows)] = share.reshape(
            span // rows, rows, inner).astype(BF16)
    each_block(right_share)
    each_peer(lambda p: send(gr_send, p, gr_recv, gr_s, gr_r, p))

    each_peer(lambda p: wait_recv(bt_all, bt_s, bt_r, p))

    def right_of(start):
        return bt_all[pl.ds(start // rows, span // rows)].astype(F32).reshape(span, inner)

    def put_u(u):
        for d in range(chans):
            for i in range(rows):
                u_mat[i * seqs:(i + 1) * seqs, d * depth:(d + 1) * depth] = u[
                    d * seqs:(d + 1) * seqs, i * depth:(i + 1) * depth].astype(BF16)

    def u_of(start):
        return dot(right_of(start).T.astype(BF16), grad_of(start))

    if blocks == 1:
        put_u(u_of(0))
    else:
        u_acc[...] = jnp.zeros_like(u_acc)

        def add_u(start):
            u_acc[...] += u_of(start)
        each_block(add_u)
        put_u(u_acc)

    share_rows = gw_send.shape[1]
    a_t = a.astype(F32).T.astype(BF16)
    gw_scale = 1.0 / (seqs * residues)
    for d in range(chans):
        part = (dot(a_t, u_mat[:, d * depth:(d + 1) * depth]) * gw_scale)
        if share_rows >= chans:
            slot, off = divmod(d * chans, share_rows)
            gw_send[slot, off:off + chans, :] = part.astype(BF16)
        else:
            per = chans // share_rows
            gw_send[d * per:(d + 1) * per] = part.reshape(per, share_rows, depth).astype(BF16)
    each_peer(lambda p: send(gw_send, p, gw_recv, gw_s, gw_r, p))

    bias_f = jnp.broadcast_to(bias[...].astype(F32), (span, depth))

    def pair_of(start):
        pair = dot(right_of(start).astype(BF16), t_mat[...])
        for i in range(rows):
            pair_out[i, pl.ds(start, span), :] = (
                pair[:, i * depth:(i + 1) * depth] * scale + bias_f).astype(BF16)
    each_block(pair_of)

    each_peer(lambda p: wait_recv(gw_recv, gw_s, gw_r, p))
    gw_recv[me] = gw_send[me]
    total = lax.fori_loop(
        0, n, lambda k, acc: acc + gw_recv[k].astype(F32),
        jnp.zeros((share_rows, depth), F32))
    gw_all[me] = total.astype(BF16)
    each_peer(lambda p: send(gw_all, me, gw_all, ga_s, ga_r, p))

    gl = dot(u_mat[...], weight_r[...], NT) * scale
    for i in range(rows):
        gl_out[:, i * chans:(i + 1) * chans] = gl[i * seqs:(i + 1) * seqs]

    each_peer(lambda p: wait_recv(gr_recv, gr_s, gr_r, p))
    gr_recv[me] = gr_send[me]
    gr = lax.fori_loop(
        0, n, lambda k, acc: acc + gr_recv[k].astype(F32), jnp.zeros((rows, inner), F32))
    wide = jnp.broadcast_to(gr[:, None, :], (rows, chans, inner)).reshape(rows * chans, inner)
    wide = jnp.where(own, wide, 0.0)
    high = wide.astype(BF16)
    low = (wide - high.astype(F32)).astype(BF16)
    gr_out[...] = dot(pick, high, NT) + dot(pick, low, NT)

    each_peer(lambda p: wait_recv(gb_all, gb_s, gb_r, p))
    gb_total = lax.fori_loop(
        0, n, lambda k, acc: acc + gb_all[k], jnp.zeros((8, depth), F32))
    gb_out[...] = jnp.sum(gb_total, axis=0, keepdims=True) * (1.0 / residues)

    each_peer(lambda p: wait_recv(gw_all, ga_s, ga_r, p))
    for d in range(chans):
        if share_rows >= chans:
            slot, off = divmod(d * chans, share_rows)
            part = gw_all[slot, off:off + chans, :].astype(F32)
        else:
            per = chans // share_rows
            part = gw_all[d * per:(d + 1) * per].astype(F32).reshape(chans, depth)
        gw_out[pl.ds(d, chans, stride=chans), :] = part

    def finish(p):
        wait_send(bt_all, bt_s, bt_r, me, p)
        wait_send(gb_all, gb_s, gb_r, me, p)
        wait_send(gr_send, gr_s, gr_r, p, p)
        wait_send(gw_send, gw_s, gw_r, p, p)
        wait_send(gw_all, ga_s, ga_r, me, p)
    each_peer(finish)


def body(n, left, right, grad, weight, bias):
    seqs = left.shape[0]
    rows, residues, depth = grad.shape
    width = weight.shape[0]
    chans = left.shape[1] // rows
    inner = chans * seqs
    vmem = pl.BlockSpec(memory_space=pltpu.VMEM)
    sem = pltpu.SemaphoreType.DMA((n,))
    blocks = max(residues // 128, 1)
    acc_shape = (inner, rows * depth) if blocks > 1 else (8, 128)
    pair, gl, gr, gw, gb = pl.pallas_call(
        functools.partial(kernel, n),
        out_shape=(
            jax.ShapeDtypeStruct((rows, residues, depth), BF16),
            jax.ShapeDtypeStruct((seqs, rows * chans), F32),
            jax.ShapeDtypeStruct((seqs, rows * chans), F32),
            jax.ShapeDtypeStruct((width, depth), F32),
            jax.ShapeDtypeStruct((1, depth), F32),
        ),
        in_specs=[vmem] * 5,
        out_specs=[vmem] * 5,
        scratch_shapes=[
            pltpu.VMEM((width, depth), F32),
            pltpu.VMEM((chans, chans * depth), BF16),
            pltpu.VMEM((inner, rows * depth), BF16),
            pltpu.VMEM((rows * seqs, chans * depth), BF16),
            pltpu.VMEM(acc_shape, F32),
            pltpu.VMEM((n, rows, inner), BF16),
            pltpu.VMEM((n, 8, depth), F32),
            pltpu.VMEM((n, rows, inner), BF16),
            pltpu.VMEM((n, rows, inner), BF16),
            pltpu.VMEM((n, width // n, depth), BF16),
            pltpu.VMEM((n, width // n, depth), BF16),
            pltpu.VMEM((n, width // n, depth), BF16),
        ] + [sem] * 10,
        compiler_params=pltpu.CompilerParams(
            collective_id=0, has_side_effects=True, vmem_limit_bytes=56 * 1024 * 1024),
    )(left, right, grad, weight, bias.reshape(1, depth))
    return pair, gl, gr, gw, gb.reshape(depth)


def solution(mesh):
    in_specs = (P("groups", "row"), P("groups", "row"), P(("groups", "row"), None, None), P(), P())
    out_specs = (
        P(("groups", "row"), None, None),
        P("groups", "row"),
        P("groups", "row"),
        P("groups", None),
        P("groups"),
    )
    return jax.shard_map(
        functools.partial(body, mesh.shape["row"]),
        mesh=mesh, in_specs=in_specs, out_specs=out_specs, check_vma=False)
```

```python
import functools

import jax
import jax.numpy as jnp
from jax import lax
from jax.experimental import pallas as pl
from jax.experimental.pallas import tpu as pltpu
from jax.sharding import PartitionSpec as P

F32, BF16 = jnp.float32, jnp.bfloat16
NN = (((1,), (0,)), ((), ()))
NT = (((1,), (1,)), ((), ()))
TN = (((0,), (0,)), ((), ()))


def dot(x, y, dims=NN):
    return lax.dot_general(x, y, dims, preferred_element_type=F32)


def kernel(
    n, left, right, grad, weight, bias,
    pair_out, gl_out, gr_out, gw_out, gb_out,
    weight_f, weight_r, t_mat, u_mat, u_acc,
    bt_all, gb_own, gb_sib, gb_all, gr_part, gr_sib, gr_send, gr_recv,
    gw_part, gw_sib, gw_send, gw_recv, gw_all,
    bt_s, bt_r, bt_f, gb_s, gb_r, gr_s, gr_r, gw_s, gw_r, ga_s, ga_r, ga_f, sib_s, sib_r,
):
    seqs = left.shape[0]
    rows, residues, depth = grad.shape
    chans = left.shape[1] // rows
    inner = chans * seqs
    span = min(128, residues)
    blocks = residues // span
    chips = n // 2
    me = lax.axis_index("row")
    chip, core = me // 2, lax.rem(me, 2)
    other = 1 - core
    sibling = chip * 2 + other

    def each_chip(action):
        def step(k, carry):
            action(lax.rem(chip + k, chips))
            return carry
        lax.fori_loop(1, chips, step, 0)

    def each_block(action):
        if blocks == 1:
            action(0)
        else:
            def step(k, carry):
                action(pl.multiple_of(k * span, span))
                return carry
            lax.fori_loop(0, blocks, step, 0)

    def copy(src, dst, sent, received, device):
        return pltpu.make_async_remote_copy(
            src_ref=src, dst_ref=dst, send_sem=sent, recv_sem=received,
            device_id={"row": device}, device_id_type=pl.DeviceIdType.MESH)

    def share(src, dst, sent, received, p):
        return copy(src.at[p], dst.at[chip], sent.at[p], received.at[chip], p * 2 + core)

    def share_in(src, dst, sent, received, p):
        return copy(src.at[p], dst.at[p], sent.at[p], received.at[p], p * 2 + core)

    def spread_to(buf, sent, received, p):
        mine = buf.at[core, chip]
        return copy(mine, mine, sent.at[p], received.at[core, chip], p * 2 + core)

    def spread_in(buf, sent, received, p):
        slot = buf.at[core, p]
        return copy(slot, slot, sent.at[p], received.at[core, p], p * 2 + core)

    def forward(buf, sent, received, p):
        slot = buf.at[core, p]
        return copy(slot, slot, sent.at[p], received.at[core, p], sibling)

    def forward_in(buf, sent, received, p):
        slot = buf.at[other, p]
        return copy(slot, slot, sent.at[p], received.at[other, p], sibling)

    def gather_start(buf, sent, received, forwarded):
        each_chip(lambda p: spread_to(buf, sent, received, p).start())
        forward(buf, forwarded, received, chip).start()

    def gather_end(buf, sent, received, forwarded):
        def arrive(p):
            spread_in(buf, sent, received, p).wait_recv()
            forward(buf, forwarded, received, p).start()
        each_chip(arrive)
        forward_in(buf, forwarded, received, chip).wait_recv()
        each_chip(lambda p: forward_in(buf, forwarded, received, p).wait_recv())

    def gather_sent(buf, sent, received, forwarded):
        each_chip(lambda p: spread_to(buf, sent, received, p).wait_send())
        each_chip(lambda p: forward(buf, forwarded, received, p).wait_send())
        forward(buf, forwarded, received, chip).wait_send()

    barrier = pltpu.get_barrier_semaphore()

    def greet(device):
        pl.semaphore_signal(
            barrier, inc=1, device_id={"row": device}, device_id_type=pl.DeviceIdType.MESH)
    each_chip(lambda p: greet(p * 2 + core))
    greet(sibling)

    lane_s = lax.broadcasted_iota(jnp.int32, (seqs, inner), 1) % seqs
    pick = (lane_s == lax.broadcasted_iota(jnp.int32, (seqs, inner), 0)).astype(BF16)
    lane_d = lax.broadcasted_iota(jnp.int32, (rows * chans, inner), 1) // seqs
    row_d = lax.broadcasted_iota(jnp.int32, (rows * chans, inner), 0) % chans
    own = lane_d == row_d
    spread = jnp.where(own, dot(right[...], pick, TN), 0.0)
    bt_all[core, chip] = jnp.sum(spread.reshape(rows, chans, inner), axis=1).astype(BF16)

    pl.semaphore_wait(barrier, chips)
    gather_start(bt_all, bt_s, bt_r, bt_f)

    gb = jnp.zeros((8, depth), F32)
    for i in range(rows):
        gb = gb + jnp.sum(grad[i].astype(F32).reshape(residues // 8, 8, depth), axis=0)
    gb_own[...] = gb
    gb_copy = copy(gb_own, gb_sib, sib_s.at[0], sib_r.at[0], sibling)
    gb_copy.start()

    a = jnp.concatenate([left[:, i * chans:(i + 1) * chans] for i in range(rows)], axis=0)
    weight_f[...] = weight[...].astype(F32)
    for d in range(chans):
        weight_r[:, d * depth:(d + 1) * depth] = weight_f[
            pl.ds(d, chans, stride=chans), :].astype(BF16)

    for d in range(chans):
        t = dot(a, weight_r[:, d * depth:(d + 1) * depth]).astype(BF16)
        for i in range(rows):
            t_mat[d * seqs:(d + 1) * seqs, i * depth:(i + 1) * depth] = (
                t[i * seqs:(i + 1) * seqs])

    def grad_of(start):
        return jnp.concatenate(
            [grad[i, pl.ds(start, span), :] for i in range(rows)], axis=1)

    scale = 1.0 / seqs
    pairs = span // (2 * rows)

    def right_share(start):
        part = dot(grad_of(start), t_mat[...], NT) * scale
        for k in range(pairs):
            for c in range(2):
                first = (2 * k + c) * rows
                gr_part[c, start // (2 * rows) + k] = part[first:first + rows]
    each_block(right_share)
    gr_copy = copy(gr_part.at[other], gr_sib, sib_s.at[1], sib_r.at[1], sibling)
    gr_copy.start()

    gather_end(bt_all, bt_s, bt_r, bt_f)

    def right_of(start):
        first = start // (2 * rows)
        halves = [bt_all[c, pl.ds(first, pairs)].astype(F32) for c in range(2)]
        return jnp.stack(halves, axis=1).reshape(span, inner)

    def put_u(u):
        for d in range(chans):
            for i in range(rows):
                u_mat[i * seqs:(i + 1) * seqs, d * depth:(d + 1) * depth] = u[
                    d * seqs:(d + 1) * seqs, i * depth:(i + 1) * depth].astype(BF16)

    def u_of(start):
        return dot(right_of(start).T.astype(BF16), grad_of(start))

    if blocks == 1:
        put_u(u_of(0))
    else:
        u_acc[...] = jnp.zeros_like(u_acc)

        def add_u(start):
            u_acc[...] += u_of(start)
        each_block(add_u)
        put_u(u_acc)

    share_rows = gw_send.shape[1]
    a_t = a.astype(F32).T.astype(BF16)
    gw_scale = 1.0 / (seqs * residues)
    for d in range(chans):
        part = (dot(a_t, u_mat[:, d * depth:(d + 1) * depth]) * gw_scale)
        half, local = divmod(d, chans // 2)
        if share_rows >= chans:
            slot, off = divmod(local * chans, share_rows)
            gw_part[half, slot, off:off + chans, :] = part
        else:
            per = chans // share_rows
            gw_part[half, local * per:(local + 1) * per] = part.reshape(per, share_rows, depth)
    gw_copy = copy(gw_part.at[other], gw_sib, sib_s.at[2], sib_r.at[2], sibling)
    gw_copy.start()

    gr_copy.wait_recv()

    def chip_gr(p):
        gr_send[p] = (gr_part[core, p] + gr_sib[p]).astype(BF16)
        share(gr_send, gr_recv, gr_s, gr_r, p).start()

    gw_copy.wait_recv()

    def chip_gw(p):
        gw_send[p] = (gw_part[core, p] + gw_sib[p]).astype(BF16)
        share(gw_send, gw_recv, gw_s, gw_r, p).start()
    each_chip(chip_gw)
    each_chip(chip_gr)

    gb_copy.wait_recv()
    gb_all[chip] = gb_own[...] + gb_sib[...]
    each_chip(lambda p: copy(
        gb_all.at[chip], gb_all.at[chip], gb_s.at[p], gb_r.at[chip], p * 2 + core).start())

    bias_f = jnp.broadcast_to(bias[...].astype(F32), (span, depth))

    def pair_of(start):
        pair = dot(right_of(start).astype(BF16), t_mat[...])
        for i in range(rows):
            pair_out[i, pl.ds(start, span), :] = (
                pair[:, i * depth:(i + 1) * depth] * scale + bias_f).astype(BF16)
    each_block(pair_of)

    def add_in(recv, sent, received, send_buf):
        def step(k, acc):
            p = lax.rem(chip + k, chips)
            share_in(send_buf, recv, sent, received, p).wait_recv()
            return acc + recv[p].astype(F32)
        return step

    total = lax.fori_loop(
        1, chips, add_in(gw_recv, gw_s, gw_r, gw_send), gw_part[core, chip] + gw_sib[chip])
    gw_all[core, chip] = total.astype(BF16)
    gather_start(gw_all, ga_s, ga_r, ga_f)

    gl = dot(u_mat[...], weight_r[...], NT) * scale
    for i in range(rows):
        gl_out[:, i * chans:(i + 1) * chans] = gl[i * seqs:(i + 1) * seqs]

    gr = lax.fori_loop(
        1, chips, add_in(gr_recv, gr_s, gr_r, gr_send), gr_part[core, chip] + gr_sib[chip])
    wide = jnp.broadcast_to(gr[:, None, :], (rows, chans, inner)).reshape(rows * chans, inner)
    wide = jnp.where(own, wide, 0.0)
    high = wide.astype(BF16)
    low = (wide - high.astype(F32)).astype(BF16)
    gr_out[...] = dot(pick, high, NT) + dot(pick, low, NT)

    each_chip(lambda p: share_in(gb_all, gb_all, gb_s, gb_r, p).wait_recv())
    gb_total = lax.fori_loop(
        0, chips, lambda k, acc: acc + gb_all[k], jnp.zeros((8, depth), F32))
    gb_out[...] = jnp.sum(gb_total, axis=0, keepdims=True) * (1.0 / residues)

    gather_end(gw_all, ga_s, ga_r, ga_f)
    for d in range(chans):
        half, local = divmod(d, chans // 2)
        if share_rows >= chans:
            slot, off = divmod(local * chans, share_rows)
            part = gw_all[half, slot, off:off + chans, :].astype(F32)
        else:
            per = chans // share_rows
            part = gw_all[half, local * per:(local + 1) * per].astype(F32).reshape(chans, depth)
        gw_out[pl.ds(d, chans, stride=chans), :] = part

    gather_sent(bt_all, bt_s, bt_r, bt_f)
    gather_sent(gw_all, ga_s, ga_r, ga_f)
    gb_copy.wait_send()
    gr_copy.wait_send()
    gw_copy.wait_send()

    def finish(p):
        share(gr_send, gr_recv, gr_s, gr_r, p).wait_send()
        share(gw_send, gw_recv, gw_s, gw_r, p).wait_send()
        copy(gb_all.at[chip], gb_all.at[chip], gb_s.at[p], gb_r.at[chip], p * 2 + core).wait_send()
    each_chip(finish)


def body(n, left, right, grad, weight, bias):
    seqs = left.shape[0]
    rows, residues, depth = grad.shape
    width = weight.shape[0]
    chans = left.shape[1] // rows
    inner = chans * seqs
    chips = n // 2
    vmem = pl.BlockSpec(memory_space=pltpu.VMEM)
    sem = pltpu.SemaphoreType.DMA((chips,))
    sem2 = pltpu.SemaphoreType.DMA((2, chips))
    blocks = max(residues // 128, 1)
    acc_shape = (inner, rows * depth) if blocks > 1 else (8, 128)
    pair, gl, gr, gw, gb = pl.pallas_call(
        functools.partial(kernel, n),
        out_shape=(
            jax.ShapeDtypeStruct((rows, residues, depth), BF16),
            jax.ShapeDtypeStruct((seqs, rows * chans), F32),
            jax.ShapeDtypeStruct((seqs, rows * chans), F32),
            jax.ShapeDtypeStruct((width, depth), F32),
            jax.ShapeDtypeStruct((1, depth), F32),
        ),
        in_specs=[vmem] * 5,
        out_specs=[vmem] * 5,
        scratch_shapes=[
            pltpu.VMEM((width, depth), F32),
            pltpu.VMEM((chans, chans * depth), BF16),
            pltpu.VMEM((inner, rows * depth), BF16),
            pltpu.VMEM((rows * seqs, chans * depth), BF16),
            pltpu.VMEM(acc_shape, F32),
            pltpu.VMEM((2, chips, rows, inner), BF16),
            pltpu.VMEM((8, depth), F32),
            pltpu.VMEM((8, depth), F32),
            pltpu.VMEM((chips, 8, depth), F32),
            pltpu.VMEM((2, chips, rows, inner), F32),
            pltpu.VMEM((chips, rows, inner), F32),
            pltpu.VMEM((chips, rows, inner), BF16),
            pltpu.VMEM((chips, rows, inner), BF16),
            pltpu.VMEM((2, chips, width // n, depth), F32),
            pltpu.VMEM((chips, width // n, depth), F32),
            pltpu.VMEM((chips, width // n, depth), BF16),
            pltpu.VMEM((chips, width // n, depth), BF16),
            pltpu.VMEM((2, chips, width // n, depth), BF16),
            sem, sem2, sem, sem, sem, sem, sem, sem, sem, sem, sem2, sem,
            pltpu.SemaphoreType.DMA((3,)),
            pltpu.SemaphoreType.DMA((3,)),
        ],
        compiler_params=pltpu.CompilerParams(
            collective_id=0, has_side_effects=True, vmem_limit_bytes=56 * 1024 * 1024),
    )(left, right, grad, weight, bias.reshape(1, depth))
    return pair, gl, gr, gw, gb.reshape(depth)


def solution(mesh):
    in_specs = (P("groups", "row"), P("groups", "row"), P(("groups", "row"), None, None), P(), P())
    out_specs = (
        P(("groups", "row"), None, None),
        P("groups", "row"),
        P("groups", "row"),
        P("groups", None),
        P("groups"),
    )
    return jax.shard_map(
        functools.partial(body, mesh.shape["row"]),
        mesh=mesh, in_specs=in_specs, out_specs=out_specs, check_vma=False)
```

```python
import functools

import jax
import jax.numpy as jnp
from jax import lax
from jax.experimental import pallas as pl
from jax.experimental.pallas import tpu as pltpu
from jax.sharding import PartitionSpec as P

F32, BF16 = jnp.float32, jnp.bfloat16
NN = (((1,), (0,)), ((), ()))
NT = (((1,), (1,)), ((), ()))
TN = (((0,), (0,)), ((), ()))


def dot(x, y, dims=NN):
    return lax.dot_general(x, y, dims, preferred_element_type=F32)


def kernel(
    n, left, right, grad, weight, bias,
    pair_out, gl_out, gr_out, gw_out, gb_out,
    weight_f, weight_r, t_mat, u_mat, u_acc,
    bt_all, gb_own, gb_sib, gb_all, gr_part, gr_sib, gr_send, gr_recv,
    gw_part, gw_sib, gw_send, gw_recv, gw_all,
    bt_s, bt_r, bt_f, gb_s, gb_r, gr_s, gr_r, gw_s, gw_r, ga_s, ga_r, ga_f, sib_s, sib_r,
):
    seqs = left.shape[0]
    rows, residues, depth = grad.shape
    chans = left.shape[1] // rows
    inner = chans * seqs
    span = min(128, residues)
    blocks = residues // span
    chips = n // 2
    me = lax.axis_index("row")
    chip, core = me // 2, lax.rem(me, 2)
    other = 1 - core
    sibling = chip * 2 + other

    def each_chip(action):
        def step(k, carry):
            action(lax.rem(chip + k, chips))
            return carry
        lax.fori_loop(1, chips, step, 0)

    def each_block(action):
        if blocks == 1:
            action(0)
        else:
            def step(k, carry):
                action(pl.multiple_of(k * span, span))
                return carry
            lax.fori_loop(0, blocks, step, 0)

    def copy(src, dst, sent, received, device):
        return pltpu.make_async_remote_copy(
            src_ref=src, dst_ref=dst, send_sem=sent, recv_sem=received,
            device_id={"row": device}, device_id_type=pl.DeviceIdType.MESH)

    def share(src, dst, sent, received, p):
        return copy(src.at[p], dst.at[chip], sent.at[p], received.at[chip], p * 2 + core)

    def share_in(src, dst, sent, received, p):
        return copy(src.at[p], dst.at[p], sent.at[p], received.at[p], p * 2 + core)

    def spread_to(buf, sent, received, p):
        mine = buf.at[core, chip]
        return copy(mine, mine, sent.at[p], received.at[core, chip], p * 2 + core)

    def spread_in(buf, sent, received, p):
        slot = buf.at[core, p]
        return copy(slot, slot, sent.at[p], received.at[core, p], p * 2 + core)

    def forward(buf, sent, received, p):
        slot = buf.at[core, p]
        return copy(slot, slot, sent.at[p], received.at[core, p], sibling)

    def forward_in(buf, sent, received, p):
        slot = buf.at[other, p]
        return copy(slot, slot, sent.at[p], received.at[other, p], sibling)

    def gather_start(buf, sent, received, forwarded):
        each_chip(lambda p: spread_to(buf, sent, received, p).start())
        forward(buf, forwarded, received, chip).start()

    def gather_end(buf, sent, received, forwarded):
        def arrive(p):
            spread_in(buf, sent, received, p).wait_recv()
            forward(buf, forwarded, received, p).start()
        each_chip(arrive)
        forward_in(buf, forwarded, received, chip).wait_recv()
        each_chip(lambda p: forward_in(buf, forwarded, received, p).wait_recv())

    def gather_sent(buf, sent, received, forwarded):
        each_chip(lambda p: spread_to(buf, sent, received, p).wait_send())
        each_chip(lambda p: forward(buf, forwarded, received, p).wait_send())
        forward(buf, forwarded, received, chip).wait_send()

    barrier = pltpu.get_barrier_semaphore()

    def greet(device):
        pl.semaphore_signal(
            barrier, inc=1, device_id={"row": device}, device_id_type=pl.DeviceIdType.MESH)
    each_chip(lambda p: greet(p * 2 + core))
    greet(sibling)

    lane_s = lax.broadcasted_iota(jnp.int32, (seqs, inner), 1) % seqs
    pick = (lane_s == lax.broadcasted_iota(jnp.int32, (seqs, inner), 0)).astype(BF16)
    lane_d = lax.broadcasted_iota(jnp.int32, (rows * chans, inner), 1) // seqs
    row_d = lax.broadcasted_iota(jnp.int32, (rows * chans, inner), 0) % chans
    own = lane_d == row_d
    spread = jnp.where(own, dot(right[...], pick, TN), 0.0)
    bt_all[core, chip] = jnp.sum(spread.reshape(rows, chans, inner), axis=1).astype(BF16)

    gb = jnp.zeros((8, depth), F32)
    for i in range(rows):
        gb = gb + jnp.sum(grad[i].astype(F32).reshape(residues // 8, 8, depth), axis=0)
    gb_own[...] = gb
    gb_copy = copy(gb_own, gb_sib, sib_s.at[0], sib_r.at[0], sibling)

    a = jnp.concatenate([left[:, i * chans:(i + 1) * chans] for i in range(rows)], axis=0)
    weight_f[...] = weight[...].astype(F32)
    for d in range(chans):
        weight_r[:, d * depth:(d + 1) * depth] = weight_f[
            pl.ds(d, chans, stride=chans), :].astype(BF16)

    for d in range(chans):
        t = dot(a, weight_r[:, d * depth:(d + 1) * depth]).astype(BF16)
        for i in range(rows):
            t_mat[d * seqs:(d + 1) * seqs, i * depth:(i + 1) * depth] = (
                t[i * seqs:(i + 1) * seqs])

    def grad_of(start):
        return jnp.concatenate(
            [grad[i, pl.ds(start, span), :] for i in range(rows)], axis=1)

    scale = 1.0 / seqs
    pairs = span // (2 * rows)

    def right_share(start):
        part = dot(grad_of(start), t_mat[...], NT) * scale
        for k in range(pairs):
            for c in range(2):
                first = (2 * k + c) * rows
                gr_part[c, start // (2 * rows) + k] = part[first:first + rows]
    each_block(right_share)
    pl.semaphore_wait(barrier, chips)
    gather_start(bt_all, bt_s, bt_r, bt_f)

    gb_copy.start()
    gr_copy = copy(gr_part.at[other], gr_sib, sib_s.at[1], sib_r.at[1], sibling)
    gr_copy.start()

    gather_end(bt_all, bt_s, bt_r, bt_f)
    gr_copy.wait_recv()

    def chip_gr(p):
        gr_send[p] = (gr_part[core, p] + gr_sib[p]).astype(BF16)
        share(gr_send, gr_recv, gr_s, gr_r, p).start()

    each_chip(chip_gr)

    def right_of(start):
        first = start // (2 * rows)
        halves = [bt_all[c, pl.ds(first, pairs)].astype(F32) for c in range(2)]
        return jnp.stack(halves, axis=1).reshape(span, inner)

    def put_u(u):
        for d in range(chans):
            for i in range(rows):
                u_mat[i * seqs:(i + 1) * seqs, d * depth:(d + 1) * depth] = u[
                    d * seqs:(d + 1) * seqs, i * depth:(i + 1) * depth].astype(BF16)

    def u_of(start):
        return dot(right_of(start).T.astype(BF16), grad_of(start))

    if blocks == 1:
        put_u(u_of(0))
    else:
        u_acc[...] = jnp.zeros_like(u_acc)

        def add_u(start):
            u_acc[...] += u_of(start)
        each_block(add_u)
        put_u(u_acc)

    share_rows = gw_send.shape[1]
    a_t = a.astype(F32).T.astype(BF16)
    gw_scale = 1.0 / (seqs * residues)
    for d in range(chans):
        part = (dot(a_t, u_mat[:, d * depth:(d + 1) * depth]) * gw_scale)
        half, local = divmod(d, chans // 2)
        if share_rows >= chans:
            slot, off = divmod(local * chans, share_rows)
            gw_part[half, slot, off:off + chans, :] = part
        else:
            per = chans // share_rows
            gw_part[half, local * per:(local + 1) * per] = part.reshape(per, share_rows, depth)
    gw_copy = copy(gw_part.at[other], gw_sib, sib_s.at[2], sib_r.at[2], sibling)
    gw_copy.start()

    gw_copy.wait_recv()

    def chip_gw(p):
        gw_send[p] = (gw_part[core, p] + gw_sib[p]).astype(BF16)
        share(gw_send, gw_recv, gw_s, gw_r, p).start()
    each_chip(chip_gw)

    gb_copy.wait_recv()
    gb_all[chip] = gb_own[...] + gb_sib[...]
    each_chip(lambda p: copy(
        gb_all.at[chip], gb_all.at[chip], gb_s.at[p], gb_r.at[chip], p * 2 + core).start())

    bias_f = jnp.broadcast_to(bias[...].astype(F32), (span, depth))

    def pair_of(start):
        pair = dot(right_of(start).astype(BF16), t_mat[...])
        for i in range(rows):
            pair_out[i, pl.ds(start, span), :] = (
                pair[:, i * depth:(i + 1) * depth] * scale + bias_f).astype(BF16)
    each_block(pair_of)

    def add_in(recv, sent, received, send_buf):
        def step(k, acc):
            p = lax.rem(chip + k, chips)
            share_in(send_buf, recv, sent, received, p).wait_recv()
            return acc + recv[p].astype(F32)
        return step

    total = lax.fori_loop(
        1, chips, add_in(gw_recv, gw_s, gw_r, gw_send), gw_part[core, chip] + gw_sib[chip])
    gw_all[core, chip] = total.astype(BF16)
    gather_start(gw_all, ga_s, ga_r, ga_f)

    gl = dot(u_mat[...], weight_r[...], NT) * scale
    for i in range(rows):
        gl_out[:, i * chans:(i + 1) * chans] = gl[i * seqs:(i + 1) * seqs]

    gr = lax.fori_loop(
        1, chips, add_in(gr_recv, gr_s, gr_r, gr_send), gr_part[core, chip] + gr_sib[chip])
    wide = jnp.broadcast_to(gr[:, None, :], (rows, chans, inner)).reshape(rows * chans, inner)
    wide = jnp.where(own, wide, 0.0)
    high = wide.astype(BF16)
    low = (wide - high.astype(F32)).astype(BF16)
    gr_out[...] = dot(pick, high, NT) + dot(pick, low, NT)

    each_chip(lambda p: share_in(gb_all, gb_all, gb_s, gb_r, p).wait_recv())
    gb_total = lax.fori_loop(
        0, chips, lambda k, acc: acc + gb_all[k], jnp.zeros((8, depth), F32))
    gb_out[...] = jnp.sum(gb_total, axis=0, keepdims=True) * (1.0 / residues)

    gather_end(gw_all, ga_s, ga_r, ga_f)
    for d in range(chans):
        half, local = divmod(d, chans // 2)
        if share_rows >= chans:
            slot, off = divmod(local * chans, share_rows)
            part = gw_all[half, slot, off:off + chans, :].astype(F32)
        else:
            per = chans // share_rows
            part = gw_all[half, local * per:(local + 1) * per].astype(F32).reshape(chans, depth)
        gw_out[pl.ds(d, chans, stride=chans), :] = part

    gather_sent(bt_all, bt_s, bt_r, bt_f)
    gather_sent(gw_all, ga_s, ga_r, ga_f)
    gb_copy.wait_send()
    gr_copy.wait_send()
    gw_copy.wait_send()

    def finish(p):
        share(gr_send, gr_recv, gr_s, gr_r, p).wait_send()
        share(gw_send, gw_recv, gw_s, gw_r, p).wait_send()
        copy(gb_all.at[chip], gb_all.at[chip], gb_s.at[p], gb_r.at[chip], p * 2 + core).wait_send()
    each_chip(finish)


def hand_over(*refs):
    sems = refs[-1]
    count = (len(refs) - 1) // 2
    copies = [
        pltpu.make_async_copy(refs[k], refs[count + k], sems.at[k]) for k in range(count)]
    for one in copies:
        one.start()
    for one in copies:
        one.wait()


def body(n, left, right, grad, weight, bias):
    seqs = left.shape[0]
    rows, residues, depth = grad.shape
    width = weight.shape[0]
    chans = left.shape[1] // rows
    inner = chans * seqs
    chips = n // 2
    vmem = pl.BlockSpec(memory_space=pltpu.VMEM)
    sem = pltpu.SemaphoreType.DMA((chips,))
    sem2 = pltpu.SemaphoreType.DMA((2, chips))
    blocks = max(residues // 128, 1)
    acc_shape = (inner, rows * depth) if blocks > 1 else (8, 128)
    outs = pl.pallas_call(
        functools.partial(kernel, n),
        out_shape=(
            jax.ShapeDtypeStruct((rows, residues, depth), BF16),
            jax.ShapeDtypeStruct((seqs, rows * chans), F32),
            jax.ShapeDtypeStruct((seqs, rows * chans), F32),
            jax.ShapeDtypeStruct((width, depth), F32),
            jax.ShapeDtypeStruct((1, depth), F32),
        ),
        in_specs=[vmem] * 5,
        out_specs=[vmem] * 5,
        scratch_shapes=[
            pltpu.VMEM((width, depth), F32),
            pltpu.VMEM((chans, chans * depth), BF16),
            pltpu.VMEM((inner, rows * depth), BF16),
            pltpu.VMEM((rows * seqs, chans * depth), BF16),
            pltpu.VMEM(acc_shape, F32),
            pltpu.VMEM((2, chips, rows, inner), BF16),
            pltpu.VMEM((8, depth), F32),
            pltpu.VMEM((8, depth), F32),
            pltpu.VMEM((chips, 8, depth), F32),
            pltpu.VMEM((2, chips, rows, inner), F32),
            pltpu.VMEM((chips, rows, inner), F32),
            pltpu.VMEM((chips, rows, inner), BF16),
            pltpu.VMEM((chips, rows, inner), BF16),
            pltpu.VMEM((2, chips, width // n, depth), F32),
            pltpu.VMEM((chips, width // n, depth), F32),
            pltpu.VMEM((chips, width // n, depth), BF16),
            pltpu.VMEM((chips, width // n, depth), BF16),
            pltpu.VMEM((2, chips, width // n, depth), BF16),
            sem, sem2, sem, sem, sem, sem, sem, sem, sem, sem, sem2, sem,
            pltpu.SemaphoreType.DMA((3,)),
            pltpu.SemaphoreType.DMA((3,)),
        ],
        compiler_params=pltpu.CompilerParams(
            collective_id=0, has_side_effects=True, vmem_limit_bytes=56 * 1024 * 1024),
    )(left, right, grad, weight, bias.reshape(1, depth))
    hbm = pl.BlockSpec(memory_space=pltpu.VMEM)
    pair, gl, gr, gw, gb = pl.pallas_call(
        hand_over,
        out_shape=tuple(jax.ShapeDtypeStruct(x.shape, x.dtype) for x in outs),
        in_specs=[pl.BlockSpec(memory_space=pl.ANY)] * 5,
        out_specs=[hbm] * 5,
        scratch_shapes=[pltpu.SemaphoreType.DMA((5,))],
    )(*outs)
    return pair, gl, gr, gw, gb.reshape(depth)


def solution(mesh):
    in_specs = (P("groups", "row"), P("groups", "row"), P(("groups", "row"), None, None), P(), P())
    out_specs = (
        P(("groups", "row"), None, None),
        P("groups", "row"),
        P("groups", "row"),
        P("groups", None),
        P("groups"),
    )
    return jax.shard_map(
        functools.partial(body, mesh.shape["row"]),
        mesh=mesh, in_specs=in_specs, out_specs=out_specs, check_vma=False)
```

```python
import functools

import jax
import jax.numpy as jnp
from jax import lax
from jax.experimental import pallas as pl
from jax.experimental.pallas import tpu as pltpu
from jax.sharding import PartitionSpec as P

F32, BF16 = jnp.float32, jnp.bfloat16
NN = (((1,), (0,)), ((), ()))
NT = (((1,), (1,)), ((), ()))
TN = (((0,), (0,)), ((), ()))


def dot(x, y, dims=NN):
    return lax.dot_general(x, y, dims, preferred_element_type=F32)


def kernel(
    n, left_in, right_in, grad_in, weight_in, bias_in,
    pair_out, gl_out, gr_out, gw_out, gb_out,
    weight_f, weight_r, t_mat, u_mat, u_acc,
    bt_all, gb_own, gb_sib, gb_all, gr_part, gr_sib, gr_send, gr_recv,
    gw_part, gw_sib, gw_send, gw_recv, gw_all,
    bt_s, bt_r, bt_f, gb_s, gb_r, gr_s, gr_r, gw_s, gw_r, ga_s, ga_r, ga_f, sib_s, sib_r,
    left, right, grad, weight, bias, load_s,
):
    seqs = left.shape[0]
    rows, residues, depth = grad.shape
    chans = left.shape[1] // rows
    inner = chans * seqs
    span = min(128, residues)
    blocks = residues // span
    chips = n // 2
    me = lax.axis_index("row")
    chip, core = me // 2, lax.rem(me, 2)
    other = 1 - core
    sibling = chip * 2 + other

    def each_chip(action):
        def step(k, carry):
            action(lax.rem(chip + k, chips))
            return carry
        lax.fori_loop(1, chips, step, 0)

    def each_block(action):
        if blocks == 1:
            action(0)
        else:
            def step(k, carry):
                action(pl.multiple_of(k * span, span))
                return carry
            lax.fori_loop(0, blocks, step, 0)

    def copy(src, dst, sent, received, device):
        return pltpu.make_async_remote_copy(
            src_ref=src, dst_ref=dst, send_sem=sent, recv_sem=received,
            device_id={"row": device}, device_id_type=pl.DeviceIdType.MESH)

    def share(src, dst, sent, received, p):
        return copy(src.at[p], dst.at[chip], sent.at[p], received.at[chip], p * 2 + core)

    def share_in(src, dst, sent, received, p):
        return copy(src.at[p], dst.at[p], sent.at[p], received.at[p], p * 2 + core)

    def spread_to(buf, sent, received, p):
        mine = buf.at[core, chip]
        return copy(mine, mine, sent.at[p], received.at[core, chip], p * 2 + core)

    def spread_in(buf, sent, received, p):
        slot = buf.at[core, p]
        return copy(slot, slot, sent.at[p], received.at[core, p], p * 2 + core)

    def forward(buf, sent, received, p):
        slot = buf.at[core, p]
        return copy(slot, slot, sent.at[p], received.at[core, p], sibling)

    def forward_in(buf, sent, received, p):
        slot = buf.at[other, p]
        return copy(slot, slot, sent.at[p], received.at[other, p], sibling)

    def gather_start(buf, sent, received, forwarded):
        each_chip(lambda p: spread_to(buf, sent, received, p).start())
        forward(buf, forwarded, received, chip).start()

    def gather_end(buf, sent, received, forwarded):
        def arrive(p):
            spread_in(buf, sent, received, p).wait_recv()
            forward(buf, forwarded, received, p).start()
        each_chip(arrive)
        forward_in(buf, forwarded, received, chip).wait_recv()
        each_chip(lambda p: forward_in(buf, forwarded, received, p).wait_recv())

    def gather_sent(buf, sent, received, forwarded):
        each_chip(lambda p: spread_to(buf, sent, received, p).wait_send())
        each_chip(lambda p: forward(buf, forwarded, received, p).wait_send())
        forward(buf, forwarded, received, chip).wait_send()

    barrier = pltpu.get_barrier_semaphore()

    def greet(device):
        pl.semaphore_signal(
            barrier, inc=1, device_id={"row": device}, device_id_type=pl.DeviceIdType.MESH)
    each_chip(lambda p: greet(p * 2 + core))
    greet(sibling)

    loads = [
        pltpu.make_async_copy(source, target, load_s.at[k])
        for k, (source, target) in enumerate((
            (right_in, right), (weight_in, weight), (left_in, left), (grad_in, grad),
            (bias_in, bias)))]
    for load in loads:
        load.start()

    loads[0].wait()

    lane_s = lax.broadcasted_iota(jnp.int32, (seqs, inner), 1) % seqs
    pick = (lane_s == lax.broadcasted_iota(jnp.int32, (seqs, inner), 0)).astype(BF16)
    lane_d = lax.broadcasted_iota(jnp.int32, (rows * chans, inner), 1) // seqs
    row_d = lax.broadcasted_iota(jnp.int32, (rows * chans, inner), 0) % chans
    own = lane_d == row_d
    spread = jnp.where(own, dot(right[...], pick, TN), 0.0)
    bt_all[core, chip] = jnp.sum(spread.reshape(rows, chans, inner), axis=1).astype(BF16)

    pl.semaphore_wait(barrier, chips)
    gather_start(bt_all, bt_s, bt_r, bt_f)

    loads[1].wait()
    loads[2].wait()
    a = jnp.concatenate([left[:, i * chans:(i + 1) * chans] for i in range(rows)], axis=0)
    weight_f[...] = weight[...].astype(F32)
    for d in range(chans):
        weight_r[:, d * depth:(d + 1) * depth] = weight_f[
            pl.ds(d, chans, stride=chans), :].astype(BF16)

    for d in range(chans):
        t = dot(a, weight_r[:, d * depth:(d + 1) * depth]).astype(BF16)
        for i in range(rows):
            t_mat[d * seqs:(d + 1) * seqs, i * depth:(i + 1) * depth] = (
                t[i * seqs:(i + 1) * seqs])

    loads[3].wait()
    loads[4].wait()
    gb = jnp.zeros((8, depth), F32)
    for i in range(rows):
        gb = gb + jnp.sum(grad[i].astype(F32).reshape(residues // 8, 8, depth), axis=0)
    gb_own[...] = gb
    gb_copy = copy(gb_own, gb_sib, sib_s.at[0], sib_r.at[0], sibling)

    def grad_of(start):
        return jnp.concatenate(
            [grad[i, pl.ds(start, span), :] for i in range(rows)], axis=1)

    scale = 1.0 / seqs
    pairs = span // (2 * rows)

    def right_share(start):
        part = dot(grad_of(start), t_mat[...], NT) * scale
        for k in range(pairs):
            for c in range(2):
                first = (2 * k + c) * rows
                gr_part[c, start // (2 * rows) + k] = part[first:first + rows]
    each_block(right_share)
    gb_copy.start()
    gr_copy = copy(gr_part.at[other], gr_sib, sib_s.at[1], sib_r.at[1], sibling)
    gr_copy.start()

    gather_end(bt_all, bt_s, bt_r, bt_f)
    gr_copy.wait_recv()

    def chip_gr(p):
        gr_send[p] = (gr_part[core, p] + gr_sib[p]).astype(BF16)
        share(gr_send, gr_recv, gr_s, gr_r, p).start()

    each_chip(chip_gr)

    def right_of(start):
        first = start // (2 * rows)
        halves = [bt_all[c, pl.ds(first, pairs)].astype(F32) for c in range(2)]
        return jnp.stack(halves, axis=1).reshape(span, inner)

    def put_u(u):
        for d in range(chans):
            for i in range(rows):
                u_mat[i * seqs:(i + 1) * seqs, d * depth:(d + 1) * depth] = u[
                    d * seqs:(d + 1) * seqs, i * depth:(i + 1) * depth].astype(BF16)

    def u_of(start):
        return dot(right_of(start).T.astype(BF16), grad_of(start))

    if blocks == 1:
        put_u(u_of(0))
    else:
        u_acc[...] = jnp.zeros_like(u_acc)

        def add_u(start):
            u_acc[...] += u_of(start)
        each_block(add_u)
        put_u(u_acc)

    share_rows = gw_send.shape[1]
    a_t = a.astype(F32).T.astype(BF16)
    gw_scale = 1.0 / (seqs * residues)
    for d in range(chans):
        part = (dot(a_t, u_mat[:, d * depth:(d + 1) * depth]) * gw_scale)
        half, local = divmod(d, chans // 2)
        if share_rows >= chans:
            slot, off = divmod(local * chans, share_rows)
            gw_part[half, slot, off:off + chans, :] = part
        else:
            per = chans // share_rows
            gw_part[half, local * per:(local + 1) * per] = part.reshape(per, share_rows, depth)
    gw_copy = copy(gw_part.at[other], gw_sib, sib_s.at[2], sib_r.at[2], sibling)
    gw_copy.start()

    gw_copy.wait_recv()

    def chip_gw(p):
        gw_send[p] = (gw_part[core, p] + gw_sib[p]).astype(BF16)
        share(gw_send, gw_recv, gw_s, gw_r, p).start()
    each_chip(chip_gw)

    gb_copy.wait_recv()
    gb_all[chip] = gb_own[...] + gb_sib[...]
    each_chip(lambda p: copy(
        gb_all.at[chip], gb_all.at[chip], gb_s.at[p], gb_r.at[chip], p * 2 + core).start())

    bias_f = jnp.broadcast_to(bias[...].astype(F32), (span, depth))

    def pair_of(start):
        pair = dot(right_of(start).astype(BF16), t_mat[...])
        for i in range(rows):
            pair_out[i, pl.ds(start, span), :] = (
                pair[:, i * depth:(i + 1) * depth] * scale + bias_f).astype(BF16)
    each_block(pair_of)

    def add_in(recv, sent, received, send_buf):
        def step(k, acc):
            p = lax.rem(chip + k, chips)
            share_in(send_buf, recv, sent, received, p).wait_recv()
            return acc + recv[p].astype(F32)
        return step

    total = lax.fori_loop(
        1, chips, add_in(gw_recv, gw_s, gw_r, gw_send), gw_part[core, chip] + gw_sib[chip])
    gw_all[core, chip] = total.astype(BF16)
    gather_start(gw_all, ga_s, ga_r, ga_f)

    gl = dot(u_mat[...], weight_r[...], NT) * scale
    for i in range(rows):
        gl_out[:, i * chans:(i + 1) * chans] = gl[i * seqs:(i + 1) * seqs]

    gr = lax.fori_loop(
        1, chips, add_in(gr_recv, gr_s, gr_r, gr_send), gr_part[core, chip] + gr_sib[chip])
    wide = jnp.broadcast_to(gr[:, None, :], (rows, chans, inner)).reshape(rows * chans, inner)
    wide = jnp.where(own, wide, 0.0)
    high = wide.astype(BF16)
    low = (wide - high.astype(F32)).astype(BF16)
    gr_out[...] = dot(pick, high, NT) + dot(pick, low, NT)

    each_chip(lambda p: share_in(gb_all, gb_all, gb_s, gb_r, p).wait_recv())
    gb_total = lax.fori_loop(
        0, chips, lambda k, acc: acc + gb_all[k], jnp.zeros((8, depth), F32))
    gb_out[...] = jnp.sum(gb_total, axis=0, keepdims=True) * (1.0 / residues)

    gather_end(gw_all, ga_s, ga_r, ga_f)
    for d in range(chans):
        half, local = divmod(d, chans // 2)
        if share_rows >= chans:
            slot, off = divmod(local * chans, share_rows)
            part = gw_all[half, slot, off:off + chans, :].astype(F32)
        else:
            per = chans // share_rows
            part = gw_all[half, local * per:(local + 1) * per].astype(F32).reshape(chans, depth)
        gw_out[pl.ds(d, chans, stride=chans), :] = part

    gather_sent(bt_all, bt_s, bt_r, bt_f)
    gather_sent(gw_all, ga_s, ga_r, ga_f)
    gb_copy.wait_send()
    gr_copy.wait_send()
    gw_copy.wait_send()

    def finish(p):
        share(gr_send, gr_recv, gr_s, gr_r, p).wait_send()
        share(gw_send, gw_recv, gw_s, gw_r, p).wait_send()
        copy(gb_all.at[chip], gb_all.at[chip], gb_s.at[p], gb_r.at[chip], p * 2 + core).wait_send()
    each_chip(finish)


def hand_over(*refs):
    sems = refs[-1]
    count = (len(refs) - 1) // 2
    copies = [
        pltpu.make_async_copy(refs[k], refs[count + k], sems.at[k]) for k in range(count)]
    for one in copies:
        one.start()
    for one in copies:
        one.wait()


def body(n, left, right, grad, weight, bias):
    seqs = left.shape[0]
    rows, residues, depth = grad.shape
    width = weight.shape[0]
    chans = left.shape[1] // rows
    inner = chans * seqs
    chips = n // 2
    vmem = pl.BlockSpec(memory_space=pltpu.VMEM)
    sem = pltpu.SemaphoreType.DMA((chips,))
    sem2 = pltpu.SemaphoreType.DMA((2, chips))
    blocks = max(residues // 128, 1)
    acc_shape = (inner, rows * depth) if blocks > 1 else (8, 128)
    outs = pl.pallas_call(
        functools.partial(kernel, n),
        out_shape=(
            jax.ShapeDtypeStruct((rows, residues, depth), BF16),
            jax.ShapeDtypeStruct((seqs, rows * chans), F32),
            jax.ShapeDtypeStruct((seqs, rows * chans), F32),
            jax.ShapeDtypeStruct((width, depth), F32),
            jax.ShapeDtypeStruct((1, depth), F32),
        ),
        in_specs=[pl.BlockSpec(memory_space=pl.ANY)] * 5,
        out_specs=[vmem] * 5,
        scratch_shapes=[
            pltpu.VMEM((width, depth), F32),
            pltpu.VMEM((chans, chans * depth), BF16),
            pltpu.VMEM((inner, rows * depth), BF16),
            pltpu.VMEM((rows * seqs, chans * depth), BF16),
            pltpu.VMEM(acc_shape, F32),
            pltpu.VMEM((2, chips, rows, inner), BF16),
            pltpu.VMEM((8, depth), F32),
            pltpu.VMEM((8, depth), F32),
            pltpu.VMEM((chips, 8, depth), F32),
            pltpu.VMEM((2, chips, rows, inner), F32),
            pltpu.VMEM((chips, rows, inner), F32),
            pltpu.VMEM((chips, rows, inner), BF16),
            pltpu.VMEM((chips, rows, inner), BF16),
            pltpu.VMEM((2, chips, width // n, depth), F32),
            pltpu.VMEM((chips, width // n, depth), F32),
            pltpu.VMEM((chips, width // n, depth), BF16),
            pltpu.VMEM((chips, width // n, depth), BF16),
            pltpu.VMEM((2, chips, width // n, depth), BF16),
            sem, sem2, sem, sem, sem, sem, sem, sem, sem, sem, sem2, sem,
            pltpu.SemaphoreType.DMA((3,)),
            pltpu.SemaphoreType.DMA((3,)),
            pltpu.VMEM(left.shape, BF16),
            pltpu.VMEM(right.shape, BF16),
            pltpu.VMEM(grad.shape, BF16),
            pltpu.VMEM(weight.shape, BF16),
            pltpu.VMEM((1, depth), BF16),
            pltpu.SemaphoreType.DMA((5,)),
        ],
        compiler_params=pltpu.CompilerParams(
            collective_id=0, has_side_effects=True, vmem_limit_bytes=56 * 1024 * 1024),
    )(left, right, grad, weight, bias.reshape(1, depth))
    hbm = pl.BlockSpec(memory_space=pltpu.VMEM)
    pair, gl, gr, gw, gb = pl.pallas_call(
        hand_over,
        out_shape=tuple(jax.ShapeDtypeStruct(x.shape, x.dtype) for x in outs),
        in_specs=[pl.BlockSpec(memory_space=pl.ANY)] * 5,
        out_specs=[hbm] * 5,
        scratch_shapes=[pltpu.SemaphoreType.DMA((5,))],
    )(*outs)
    return pair, gl, gr, gw, gb.reshape(depth)


def solution(mesh):
    in_specs = (P("groups", "row"), P("groups", "row"), P(("groups", "row"), None, None), P(), P())
    out_specs = (
        P(("groups", "row"), None, None),
        P("groups", "row"),
        P("groups", "row"),
        P("groups", None),
        P("groups"),
    )
    return jax.shard_map(
        functools.partial(body, mesh.shape["row"]),
        mesh=mesh, in_specs=in_specs, out_specs=out_specs, check_vma=False)
```
